128 devices in a mesh: tm: 4 (over x), rows: 32 (over y, z, core).
Axes of the slice: x: 4, y: 4, z: 4, core: 2. Of those that a mesh axis runs over, the one named last changes fastest.
Arguments:
- frames: bfloat16 [16, 256, 1280, 128], P('tm', 'rows'), may hold values from -30 to 30
- clip_ids: int32 [16], replicated, may hold values from 0 to 3, never falling along the last dimension, each value on 1 to 6 neighbouring positions
- conv_weight: bfloat16 [3, 3, 3, 128, 256], replicated, may hold values from -0.109375 to 0.109375
- norm_gain: float32 [256], replicated, may hold values from 0.1 to 1.9
- norm_bias: float32 [256], replicated, may hold values from -3 to 3
Outputs:
- latent: bfloat16 [16, 128, 640, 256], P('tm', None, 'rows')
The draws below stay inside these ranges and needn't reach their ends.
Inputs may be any that keep to these rules, and one draw needn't show every extreme that they name: `clip_ids`: clip numbers never fall along the frames; each clip spans 1 to 6 frames, one exactly 6.
All inputs are finite; a program needn't handle non-finite values.
Results may differ from the reference program's by a relative error of at most 0.012.
Values may be sent and summed in bfloat16 or wider, within the bound.
A program may use at most 192 MiB of HBM per device.

```python
import math
import jax
import jax.numpy as jnp
import numpy as np
from jax import lax

CI = 128
CO = 256
GROUPS = 32
WIDTH = 1280
CLIPS = 4
CLIP_MOST = 6
NF = 16
H = 256
HO = 128
WO = 640


def draw_frames(key, part):
    key_values = jax.random.fold_in(key, 11)
    key_channels = jax.random.fold_in(key, 12)
    heights = jnp.arange(H, dtype=jnp.float32) / (H - 1)
    channel_scale = jnp.exp(jax.random.uniform(key_channels, (CI,), jnp.float32, 0.0, 1.1))
    base = jnp.clip(jax.random.normal(key_values, (NF, H, WIDTH, CI), jnp.float32), -5.0, 5.0)
    base = base * (1.0 + 2.0 * heights)[None, :, None, None]
    return (base * channel_scale * 0.5).astype(jnp.bfloat16)


def length_profile(amount, total, bound, skew):
    portions = [(1 << 20) // math.isqrt(standing ** skew) + 1 for standing in range(2, amount + 1)]
    surplus, given = total - bound - (amount - 1), [1] * (amount - 1)
    while surplus > 0:
        movable = [i for i in range(amount - 1) if given[i] < bound]
        mass, remaining = sum([portions[i] for i in movable]), surplus
        for i in movable:
            more = min(bound - given[i], max(1, remaining * portions[i] // mass), surplus)
            given[i] = given[i] + more
            surplus = surplus - more
    return np.array([bound] + given)


def ragged(rng, number_of, total, bound, skew):
    if number_of == 2:
        one = jax.random.randint(rng, (), max(1, total - bound), min(bound, total - 1) + 1)
        return jnp.stack([one, total - one])
    tallies = jnp.asarray(length_profile(number_of, total, bound, skew), jnp.int32)
    pairs = (number_of - 1) // 2
    giver, taker = tallies[1:1 + 2 * pairs:2], tallies[2:2 + 2 * pairs:2]
    margin = jnp.minimum(giver - 1, bound - taker)
    passed = jax.random.randint(jax.random.fold_in(rng, 1), (pairs,), 0, 1 << 20) % (margin + 1)
    tallies = tallies.at[1:1 + 2 * pairs:2].set(giver - passed).at[2:2 + 2 * pairs:2].set(taker + passed)
    return tallies[jax.random.permutation(jax.random.fold_in(rng, 2), number_of)]


def normal_values(own_key, extent, deviation, most, kind=jnp.bfloat16):
    return jnp.clip(deviation * jax.random.normal(own_key, extent, jnp.float32), -most, most).astype(kind)


def setup_inputs(seed: int = 0) -> dict:
    splits = jax.random.split(jax.random.key(seed), 6)
    frames = draw_frames(jax.random.fold_in(splits[5], 71), 0)
    clip_ids = jnp.searchsorted(jnp.cumsum(ragged(splits[1], CLIPS, NF, CLIP_MOST, 2)), jnp.arange(NF), side="right").astype(jnp.int32)
    conv_weight = normal_values(splits[2], (3, 3, 3, CI, CO), (27 * CI) ** -0.5, 0.109375)
    norm_gain = jnp.clip(1.0 + 0.18 * jax.random.normal(splits[3], (CO,), jnp.float32), 0.1, 1.9)
    norm_bias = normal_values(splits[4], (CO,), 0.5, 3.0, jnp.float32)
    return dict(frames=frames, clip_ids=clip_ids, conv_weight=conv_weight, norm_gain=norm_gain, norm_bias=norm_bias)


def plane_conv(image, kernel):
    return lax.conv_general_dilated(image[None], kernel.astype(jnp.float32), (2, 2), ((1, 1), (1, 1)), dimension_numbers=('NHWC', 'HWIO', 'NHWC'))[0]

def reference(frames, clip_ids, conv_weight, norm_gain, norm_bias):

    def one_frame(frame_at):
        running = jnp.zeros((HO, WO, CO), jnp.float32)
        for tap_index in range(3):
            source = frame_at - 2 + tap_index
            safe = jnp.maximum(source, 0).astype(jnp.int32)
            valid = jnp.logical_and(source >= 0, clip_ids[safe] == clip_ids[frame_at])
            image = lax.dynamic_index_in_dim(frames, safe, 0, keepdims=False).astype(jnp.float32)
            image = image * valid.astype(jnp.float32)
            running = running + plane_conv(image, conv_weight[tap_index])
        return running.astype(jnp.bfloat16)
    conv = lax.map(one_frame, jnp.arange(NF, dtype=jnp.int32))
    values = conv.astype(jnp.float32).reshape(NF, HO, WO, GROUPS, CO // GROUPS)
    mean = lax.optimization_barrier(jnp.mean(values, axis=(1, 2, 4)))
    variance = lax.optimization_barrier(jnp.mean(values * values, axis=(1, 2, 4))) - mean * mean
    scaled = (values - mean[:, None, None, :, None]) * lax.rsqrt(variance + 1e-05)[:, None, None, :, None]
    scaled = scaled.reshape(NF, HO, WO, CO) * norm_gain + norm_bias
    return jax.nn.silu(scaled).astype(jnp.bfloat16)
```

```python
import functools

import jax
import jax.numpy as jnp
from jax import lax
from jax.experimental import pallas as pl
from jax.experimental.pallas import tpu as pltpu
from jax.sharding import PartitionSpec as P

GROUPS = 32
EPS = 1e-05
MESH = pl.DeviceIdType.MESH
MIB = 2**20
FR = 4
BAND = 8
WIDTH = 1280
WO = 640
CI = 128
CO = 256
COLS = 20
PEERS = 32
TILE = 320
LEAD = 8


def repeat(count, body):
    lax.fori_loop(0, count, lambda u, c: (body(u), c)[1], 0)


def conv_kernel(
    clips, frames, weight, got, got_sums,
    rows_in, taps_in, stage, send, part_send, part_got, sums, sums_send,
    load_sem, halo_s, halo_r, part_s, part_r, out_s, out_r, sum_s, sum_r, own_sem,
):
    tm = lax.axis_index("tm")
    me = lax.axis_index("rows")
    tm_count = lax.axis_size("tm")
    tm_next = lax.rem(tm + 1, tm_count)
    tm_last = lax.rem(tm + tm_count - 1, tm_count)
    below = lax.rem(me + 1, PEERS)

    def peer(d):
        return lax.rem(me + 1 + d, PEERS)

    def load(f, part):
        first, count = ((3, 5), (0, 3))[part]
        return pltpu.make_async_copy(
            frames.at[f, pl.ds(first, count)],
            rows_in.at[f, pl.ds(first + 1, count)],
            load_sem.at[f, part],
        )

    for part in range(2):
        for f in (2, 0, 1, 3):
            load(f, part).start()

    barrier = pltpu.get_barrier_semaphore()
    repeat(
        PEERS - 1,
        lambda d: pl.semaphore_signal(barrier, inc=1, device_id=(tm, peer(d)), device_id_type=MESH),
    )
    for other in (tm_next, tm_last):
        pl.semaphore_signal(barrier, inc=1, device_id=(other, me), device_id_type=MESH)

    stage[0:LEAD] = jnp.zeros((LEAD, CI), jnp.float32)
    sums[...] = jnp.zeros(sums.shape, jnp.float32)

    above = jnp.where(me > 0, 1.0, 0.0).astype(jnp.float32)

    def split(f, first, count):
        def body(u):
            r = first + u
            row = rows_in[f, r].astype(jnp.float32)
            stage[LEAD : LEAD + WIDTH] = row if first else row * above
            for b in range(3):
                taps_in[f, r, :, b * CI : (b + 1) * CI] = stage[
                    pl.ds(LEAD - 1 + b, WO, stride=2), :
                ].astype(jnp.bfloat16)

        repeat(count, body)

    load(2, 0).wait()
    split(2, 4, 5)

    pl.semaphore_wait(barrier, PEERS + 1)

    def halo(f):
        return pltpu.make_async_remote_copy(
            frames.at[f, BAND - 1],
            rows_in.at[f, 0],
            halo_s.at[f],
            halo_r.at[f],
            device_id=(tm, below),
            device_id_type=MESH,
        )

    for f in (2, 3, 0, 1):
        halo(f).start()

    start = tm * FR

    def mask(target, source):
        inside = jnp.logical_or(tm < tm_count - 1, target < FR)
        last = tm_count * FR
        same = clips[lax.rem(start + target, last)] == clips[lax.rem(start + source, last)]
        return jnp.where(jnp.logical_and(inside, same), 1.0, 0.0).astype(jnp.float32)

    def dots(terms, row, col):
        total = None
        for f, k, m in terms:
            left = jnp.concatenate(
                [taps_in[f, 2 * row + a, pl.ds(col, TILE), :] for a in range(3)], axis=1
            )
            term = jnp.dot(left, weight[k], preferred_element_type=jnp.float32)
            if m is not None:
                term = term * m
            total = term if total is None else total + term
        return total

    def part_copy(g, n):
        return pltpu.make_async_remote_copy(
            part_send.at[g, n],
            part_got.at[g, n],
            part_s.at[g, n],
            part_r.at[g, n],
            device_id=(tm_next, me),
            device_id_type=MESH,
        )

    def partial_sums(g, n):
        if n == 0:
            terms = [(2, 0, mask(4, 2)), (3, 1, mask(4, 3))]
        else:
            terms = [(3, 0, mask(5, 3))]

        def body(u):
            r, q = u // 2, lax.rem(u, 2)
            col = pl.multiple_of(q * TILE, TILE)
            value = dots(terms, 2 - 2 * g + r, col)
            part_send[g, n, r, pl.ds(col, TILE), :] = value.astype(jnp.bfloat16)

        repeat(4, body)
        part_copy(g, n).start()

    def out_copy(t, g, to):
        return pltpu.make_async_remote_copy(
            send.at[t, g, to],
            got.at[t, g, me],
            out_s.at[t, g],
            out_r.at[t, g],
            device_id=(tm, to),
            device_id_type=MESH,
        )

    def own_copy(t, g):
        return pltpu.make_async_copy(send.at[t, g, me], got.at[t, g, me], own_sem.at[t, g])

    def outputs(t, g):
        terms = [
            (t - 2 + k, k, None if k == 2 else mask(t, t - 2 + k)) for k in range(3) if t - 2 + k >= 0
        ]

        def body(q):
            col = pl.multiple_of(q * TILE, TILE)
            row = 2 - 2 * g
            upper = dots(terms, row, col)
            lower = dots(terms, row + 1, col)
            if t < 2:
                upper = upper + part_got[g, t, 0, pl.ds(col, TILE), :].astype(jnp.float32)
                lower = lower + part_got[g, t, 1, pl.ds(col, TILE), :].astype(jnp.float32)
            by8 = (TILE // 8, 8, CO)
            sums[t, 0] += jnp.sum((upper + lower).reshape(by8), axis=0)
            sums[t, 1] += jnp.sum((upper * upper + lower * lower).reshape(by8), axis=0)
            pairs = TILE // (2 * COLS)
            upper = upper.reshape(pairs, 2 * COLS, CO)
            lower = lower.reshape(pairs, 2 * COLS, CO)
            even = jnp.concatenate([upper[:, :COLS], lower[:, :COLS]], axis=1)
            odd = jnp.concatenate([upper[:, COLS:], lower[:, COLS:]], axis=1)
            for j in range(pairs):
                to = q * (2 * pairs) + 2 * j
                send[t, g, to] = even[j].astype(jnp.bfloat16)
                send[t, g, to + 1] = odd[j].astype(jnp.bfloat16)

        repeat(2, body)
        repeat(PEERS - 1, lambda d: out_copy(t, g, peer(d)).start())
        own_copy(t, g).start()

    def sum_copy(t, to):
        return pltpu.make_async_remote_copy(
            sums_send.at[t],
            got_sums.at[t, me],
            sum_s.at[t],
            sum_r.at[t],
            device_id=(tm, to),
            device_id_type=MESH,
        )

    def own_sums(t):
        return pltpu.make_async_copy(sums_send.at[t], got_sums.at[t, me], own_sem.at[t, 2])

    def group_sums(t):
        sums_send[t] = jnp.sum(sums[t], axis=1)
        repeat(PEERS - 1, lambda d: sum_copy(t, peer(d)).start())
        own_sums(t).start()

    for f in (0, 1):
        load(f, 0).wait()
        split(f, 4, 5)
    outputs(2, 0)
    load(3, 0).wait()
    split(3, 4, 5)
    partial_sums(0, 0)
    partial_sums(0, 1)
    outputs(3, 0)
    for f in (2, 3, 0, 1):
        load(f, 1).wait()
        split(f, 1, 3)
        halo(f).wait_recv()
        split(f, 0, 1)
        if f == 3:
            partial_sums(1, 0)
            partial_sums(1, 1)
    for t in (2, 3):
        outputs(t, 1)
        group_sums(t)
    for g in range(2):
        for t in range(2):
            part_copy(g, t).wait_recv()
            outputs(t, g)
            if g == 1:
                group_sums(t)

    for f in range(FR):
        halo(f).wait_send()
    for g in range(2):
        for t in range(2):
            part_copy(g, t).wait_send()
    for t in (2, 3, 0, 1):
        for g in range(2):
            own_copy(t, g).wait()
            every = pltpu.make_async_remote_copy(
                send.at[t, g, pl.ds(0, PEERS - 1)],
                got.at[t, g, pl.ds(0, PEERS - 1)],
                out_s.at[t, g],
                out_r.at[t, g],
                device_id=(tm, below),
                device_id_type=MESH,
            )
            every.wait()
        own_sums(t).wait()
        sent = pltpu.make_async_remote_copy(
            got_sums.at[t, pl.ds(0, PEERS - 1)],
            got_sums.at[t, pl.ds(0, PEERS - 1)],
            sum_s.at[t],
            sum_r.at[t],
            device_id=(tm, below),
            device_id_type=MESH,
        )
        sent.wait()


def conv_call(clips, frames, weight):
    dma = pltpu.SemaphoreType.DMA
    return pl.pallas_call(
        conv_kernel,
        out_shape=[
            jax.ShapeDtypeStruct((FR, 2, PEERS, 2 * COLS, CO), jnp.bfloat16),
            jax.ShapeDtypeStruct((FR, PEERS, 2, CO), jnp.float32),
        ],
        in_specs=[
            pl.BlockSpec(memory_space=pltpu.SMEM),
            pl.BlockSpec(memory_space=pl.ANY),
            pl.BlockSpec(memory_space=pltpu.VMEM),
        ],
        out_specs=[pl.BlockSpec(memory_space=pl.ANY)] * 2,
        scratch_shapes=[
            pltpu.VMEM((FR, BAND + 1, WIDTH, CI), jnp.bfloat16),
            pltpu.VMEM((FR, BAND + 1, WO, 3 * CI), jnp.bfloat16),
            pltpu.VMEM((LEAD + WIDTH + 8, CI), jnp.float32),
            pltpu.VMEM((FR, 2, PEERS, 2 * COLS, CO), jnp.bfloat16),
            pltpu.VMEM((2, 2, 2, WO, CO), jnp.bfloat16),
            pltpu.VMEM((2, 2, 2, WO, CO), jnp.bfloat16),
            pltpu.VMEM((FR, 2, 8, CO), jnp.float32),
            pltpu.VMEM((FR, 2, CO), jnp.float32),
            dma((FR, 2)), dma((FR,)), dma((FR,)), dma((2, 2)), dma((2, 2)),
            dma((FR, 2)), dma((FR, 2)), dma((FR,)), dma((FR,)), dma((FR, 3)),
        ],
        compiler_params=pltpu.CompilerParams(
            collective_id=0, has_side_effects=True, vmem_limit_bytes=58 * MIB
        ),
        name="conv",
    )(clips, frames, weight)


PITCH = 136


def group_totals(sums):
    lane = lax.broadcasted_iota(jnp.int32, sums.shape, 1)
    for by in (1, 2, 4):
        up, down = pltpu.roll(sums, CO - by, 1), pltpu.roll(sums, by, 1)
        sums = sums + jnp.where(lax.rem(lane // by, 2) == 0, up, down)
    return sums


def norm_kernel(entries, got, got_sums, gain, bias, latent, columns):
    total = jnp.sum(got_sums[0], axis=0)
    total = group_totals(jnp.concatenate([total, jnp.zeros((6, CO), jnp.float32)], axis=0))
    mean = total[0:1] / entries
    variance = total[1:2] / entries - mean * mean
    scale = lax.rsqrt(variance + EPS) * gain[...]
    shift = bias[...]
    for s in range(PEERS):
        for g in range(2):
            value = got[0, g, s].astype(jnp.float32)
            half = ((value - mean) * scale + shift) * 0.5
            value = half * jnp.tanh(half) + half
            for r in range(2):
                for h in range(2):
                    columns[h, pl.ds(4 * s + 2 - 2 * g + r, COLS, stride=PITCH), :] = value[
                        r * COLS : (r + 1) * COLS, h * 128 : (h + 1) * 128
                    ]
    for j in range(COLS):
        for h in range(2):
            latent[0, j, :, h * 128 : (h + 1) * 128] = columns[
                h, pl.ds(j * PITCH, 4 * PEERS), :
            ].astype(jnp.bfloat16)


def norm_call(got, got_sums, gain, bias):
    latent = pl.pallas_call(
        functools.partial(norm_kernel, float(PEERS * 4 * WO * (CO // GROUPS))),
        grid=(FR,),
        out_shape=jax.ShapeDtypeStruct((FR, COLS, PEERS * 4, CO), jnp.bfloat16),
        in_specs=[
            pl.BlockSpec((1, 2, PEERS, 2 * COLS, CO), lambda t: (t, 0, 0, 0, 0)),
            pl.BlockSpec((1, PEERS, 2, CO), lambda t: (t, 0, 0, 0)),
            pl.BlockSpec((1, CO), lambda t: (0, 0)),
            pl.BlockSpec((1, CO), lambda t: (0, 0)),
        ],
        out_specs=pl.BlockSpec((1, COLS, PEERS * 4, CO), lambda t: (t, 0, 0, 0)),
        scratch_shapes=[pltpu.VMEM((2, COLS * PITCH, 128), jnp.float32)],
        compiler_params=pltpu.CompilerParams(vmem_limit_bytes=60 * MIB),
        name="norm",
    )(got, got_sums, gain, bias)
    return latent.transpose(0, 2, 1, 3)


def on_device(frames, clip_ids, conv_weight, norm_gain, norm_bias):
    weight = conv_weight.reshape(3, 9 * CI, CO)
    got, got_sums = conv_call(clip_ids, frames, weight)
    return norm_call(got, got_sums, norm_gain.reshape(1, CO), norm_bias.reshape(1, CO))


def solution(mesh):
    in_specs = (P("tm", "rows", None, None), P(), P(), P(), P())
    out_specs = P("tm", None, "rows", None)
    return jax.shard_map(
        on_device, mesh=mesh, in_specs=in_specs, out_specs=out_specs, check_vma=False
    )
```

```python
import functools

import jax
import jax.numpy as jnp
from jax import lax
from jax.experimental import pallas as pl
from jax.experimental.pallas import tpu as pltpu
from jax.sharding import PartitionSpec as P

GROUPS = 32
EPS = 1e-05
MESH = pl.DeviceIdType.MESH
MIB = 2**20
FR = 4
BAND = 8
WIDTH = 1280
WO = 640
CI = 128
CO = 256
COLS = 20
PEERS = 32
TILE = 320
PIECE = 160
PIECES = WIDTH // PIECE
RELAYED = ((2, 0), (3, 0))


def repeat(count, body):
    lax.fori_loop(0, count, lambda u, c: (body(u), c)[1], 0)


PITCH = 136


def group_totals(sums):
    lane = lax.broadcasted_iota(jnp.int32, sums.shape, 1)
    for by in (1, 2, 4):
        up, down = pltpu.roll(sums, CO - by, 1), pltpu.roll(sums, by, 1)
        sums = sums + jnp.where(lax.rem(lane // by, 2) == 0, up, down)
    return sums


def moments(sums, gain, entries):
    total = jnp.sum(sums, axis=0)
    total = group_totals(jnp.concatenate([total, jnp.zeros((6, CO), jnp.float32)], axis=0))
    mean = total[0:1] / entries
    variance = total[1:2] / entries - mean * mean
    return mean, lax.rsqrt(variance + EPS) * gain


def normalize(frame, sums, gain, bias, latent, columns, entries):
    mean, scale = moments(sums[...], gain[...], entries)
    scale = scale * 0.5
    shift = bias[...] * 0.5
    for s in range(PEERS):
        for g in range(2):
            half = (frame[g, s].astype(jnp.float32) - mean) * scale + shift
            value = half * jnp.tanh(half) + half
            for r in range(2):
                for h in range(2):
                    columns[h, pl.ds(4 * s + 2 - 2 * g + r, COLS, stride=PITCH), :] = value[
                        r * COLS : (r + 1) * COLS, h * 128 : (h + 1) * 128
                    ]
    for j in range(COLS):
        for h in range(2):
            latent[j, :, h * 128 : (h + 1) * 128] = columns[
                h, pl.ds(j * PITCH, 4 * PEERS), :
            ].astype(jnp.bfloat16)


def conv_kernel(
    entries, clips, frames, weight_in, gain, bias, got, got_sums, done,
    rows_in, taps_in, weight, send, part_send, part_got, sums, sums_send,
    frame, frame_sums, frame_out, columns,
    load_sem, halo_s, halo_r, part_s, part_r, out_s, out_r, sum_s, sum_r, own_sem, norm_sem, relay, relay_s, relay_r, forward_s,
):
    tm = lax.axis_index("tm")
    me = lax.axis_index("rows")
    tm_count = lax.axis_size("tm")
    tm_next = lax.rem(tm + 1, tm_count)
    tm_last = lax.rem(tm + tm_count - 1, tm_count)
    below = lax.rem(me + 1, PEERS)

    def load(f, part):
        first, count = ((3, 5), (0, 3))[part]
        return pltpu.make_async_copy(
            frames.at[f, pl.ds(first, count)],
            rows_in.at[f, pl.ds(first + 1, count)],
            load_sem.at[f, part],
        )

    load_weight = pltpu.make_async_copy(weight_in, weight, load_sem.at[FR, 0])
    load(2, 0).start()
    load(3, 0).start()
    load_weight.start()
    load(0, 0).start()
    load(1, 0).start()
    for f in (2, 3, 0, 1):
        load(f, 1).start()

    barrier = pltpu.get_barrier_semaphore()

    def greet(d):
        to = lax.rem(me + 1 + d, PEERS)
        pl.semaphore_signal(barrier, inc=1, device_id=(tm, to), device_id_type=MESH)

    repeat(PEERS - 1, greet)
    for other in (tm_next, tm_last):
        pl.semaphore_signal(barrier, inc=1, device_id=(other, me), device_id_type=MESH)

    sums[...] = jnp.zeros(sums.shape, jnp.float32)
    above = jnp.where(me > 0, 1.0, 0.0).astype(jnp.bfloat16)

    def split(f, first, count):
        def body(u):
            r = first + u
            row = rows_in[f, r]
            pairs = (row if first else row * above).reshape(WO, 2 * CI)
            taps_in[f, r, :, CI:] = pairs
            before = jnp.zeros((1, CI), jnp.bfloat16)
            taps_in[f, r, :, :CI] = jnp.concatenate([before, pairs[:-1, CI:]], axis=0)

        repeat(count, body)

    start = tm * FR

    def mask(target, source):
        inside = jnp.logical_or(tm < tm_count - 1, target < FR)
        last = tm_count * FR
        same = clips[lax.rem(start + target, last)] == clips[lax.rem(start + source, last)]
        return jnp.where(jnp.logical_and(inside, same), 1.0, 0.0).astype(jnp.float32)

    def dots(terms, row, col):
        total = None
        for f, k, m in terms:
            left = jnp.concatenate(
                [taps_in[f, 2 * row + a, pl.ds(col, TILE), :] for a in range(3)], axis=1
            )
            term = jnp.dot(left, weight[k], preferred_element_type=jnp.float32)
            if m is not None:
                term = term * m
            total = term if total is None else total + term
        return total

    def halo(f):
        return pltpu.make_async_remote_copy(
            frames.at[f, BAND - 1],
            rows_in.at[f, 0],
            halo_s.at[f],
            halo_r.at[f],
            device_id=(tm, below),
            device_id_type=MESH,
        )

    def halo_pieces(first, count):
        def body(u):
            i = first + u
            f = lax.rem(i // PIECES * 2, 4) + i // (2 * PIECES)
            at = pl.ds(pl.multiple_of(lax.rem(i, PIECES) * PIECE, PIECE), PIECE)
            pltpu.make_async_remote_copy(
                frames.at[f, BAND - 1, at],
                rows_in.at[f, 0, at],
                halo_s.at[f],
                halo_r.at[f],
                device_id=(tm, below),
                device_id_type=MESH,
            ).start()

        repeat(count, body)

    def part_copy(n, row):
        return pltpu.make_async_remote_copy(
            part_send.at[n, row],
            part_got.at[n, row],
            part_s.at[n, row],
            part_r.at[n, row],
            device_id=(tm_next, me),
            device_id_type=MESH,
        )

    def partial_sums(n, row):
        if n == 0:
            terms = [(2, 0, mask(4, 2)), (3, 1, mask(4, 3))]
        else:
            terms = [(3, 0, mask(5, 3))]

        def body(q):
            col = pl.multiple_of(q * TILE, TILE)
            part_send[n, row, pl.ds(col, TILE), :] = dots(terms, row, col).astype(jnp.bfloat16)

        repeat(2, body)
        part_copy(n, row).start()

    def out_copy(t, g, to):
        return pltpu.make_async_remote_copy(
            send.at[t, g, to],
            got.at[t, g, me],
            out_s.at[t, g],
            out_r.at[t, g],
            device_id=(tm, to),
            device_id_type=MESH,
        )

    y, z, core = me // 8, lax.rem(me // 2, 4), lax.rem(me, 2)
    z_less, z_more, z_two = lax.rem(z + 3, 4), lax.rem(z + 1, 4), lax.rem(z + 2, 4)

    def relay_copy(n, d):
        t, g = RELAYED[n]
        to = lax.rem(y + d // 2, 4) * 8 + z_two * 2 + lax.rem(core + d, 2)
        return pltpu.make_async_remote_copy(
            send.at[t, g, to],
            relay.at[n, d],
            relay_s.at[n],
            relay_r.at[n],
            device_id=(tm, y * 8 + z_less * 2 + core),
            device_id_type=MESH,
        )

    def forward(n):
        t, g = RELAYED[n]
        source = y * 8 + z_more * 2 + core
        relay_all(n).wait_recv()

        def body(d):
            to = lax.rem(y + d // 2, 4) * 8 + z_less * 2 + lax.rem(core + d, 2)
            pltpu.make_async_remote_copy(
                relay.at[n, d],
                got.at[t, g, source],
                forward_s.at[n],
                out_r.at[t, g],
                device_id=(tm, to),
                device_id_type=MESH,
            ).start()

        repeat(8, body)

    def relay_all(n):
        return pltpu.make_async_remote_copy(
            relay.at[n], relay.at[n], relay_s.at[n], relay_r.at[n],
            device_id=(tm, below), device_id_type=MESH,
        )

    def forward_all(n):
        return pltpu.make_async_remote_copy(
            relay.at[n], relay.at[n], forward_s.at[n], relay_r.at[n],
            device_id=(tm, below), device_id_type=MESH,
        )

    def own_copy(t, g):
        return pltpu.make_async_copy(send.at[t, g, me], got.at[t, g, me], own_sem.at[t, g])

    def outputs(t, g):
        terms = [
            (t - 2 + k, k, None if k == 2 else mask(t, t - 2 + k)) for k in range(3) if t - 2 + k >= 0
        ]
        row = 2 - 2 * g
        pairs = TILE // (2 * COLS)

        def body(u):
            q = lax.rem(u + z, 2)
            col = pl.multiple_of(q * TILE, TILE)
            upper = dots(terms, row, col)
            lower = dots(terms, row + 1, col)
            if t < 2:
                upper = upper + part_got[t, row, pl.ds(col, TILE), :].astype(jnp.float32)
                lower = lower + part_got[t, row + 1, pl.ds(col, TILE), :].astype(jnp.float32)
            by8 = (TILE // 8, 8, CO)
            sums[t, 0] += jnp.sum((upper + lower).reshape(by8), axis=0)
            sums[t, 1] += jnp.sum((upper * upper + lower * lower).reshape(by8), axis=0)
            upper = upper.reshape(pairs, 2 * COLS, CO)
            lower = lower.reshape(pairs, 2 * COLS, CO)
            even = jnp.concatenate([upper[:, :COLS], lower[:, :COLS]], axis=1)
            odd = jnp.concatenate([upper[:, COLS:], lower[:, COLS:]], axis=1)
            for j in range(pairs):
                to = q * (2 * pairs) + 2 * j
                send[t, g, to] = even[j].astype(jnp.bfloat16)
                send[t, g, to + 1] = odd[j].astype(jnp.bfloat16)

            if (t, g) in ((2, 0), (3, 0)):
                halo_pieces(12 + 10 * (t - 2) + 5 * u, 5)

            def push(d):
                to = q * (2 * pairs) + lax.rem(me + 1 + 3 * d, 2 * pairs)
                direct = to != me
                if (t, g) in RELAYED:
                    direct = jnp.logical_and(direct, lax.rem(to // 2, 4) != z_two)

                @pl.when(direct)
                def _():
                    out_copy(t, g, to).start()

            repeat(2 * pairs, push)

        repeat(2, body)
        own_copy(t, g).start()
        if (t, g) in RELAYED:
            repeat(8, lambda d: relay_copy(RELAYED.index((t, g)), d).start())

    def sum_copy(t, to):
        return pltpu.make_async_remote_copy(
            sums_send.at[t],
            got_sums.at[t, me],
            sum_s.at[t],
            sum_r.at[t],
            device_id=(tm, to),
            device_id_type=MESH,
        )

    def own_sums(t):
        return pltpu.make_async_copy(sums_send.at[t], got_sums.at[t, me], own_sem.at[t, 2])

    def group_sums(t):
        sums_send[t] = jnp.sum(sums[t], axis=1)
        repeat(PEERS - 1, lambda d: sum_copy(t, lax.rem(me + 1 + d, PEERS)).start())
        own_sums(t).start()

    pl.semaphore_wait(barrier, PEERS + 1)
    halo_pieces(0, 12)
    for f in (2, 3):
        load(f, 0).wait()
        split(f, 4, 5)
    load_weight.wait()
    partial_sums(0, 2)
    for f in (0, 1):
        load(f, 0).wait()
        split(f, 4, 5)
    outputs(2, 0)
    partial_sums(0, 3)
    outputs(3, 0)
    partial_sums(1, 2)
    partial_sums(1, 3)
    for f in (2, 3):
        load(f, 1).wait()
        split(f, 1, 3)
    partial_sums(0, 1)
    partial_sums(1, 1)
    for f in (0, 1):
        load(f, 1).wait()
        split(f, 1, 3)
    for f in (0, 2, 1, 3):
        halo(f).wait_recv()
    for n in range(len(RELAYED)):
        forward(n)
    for f in (0, 1, 2, 3):
        split(f, 0, 1)
    outputs(2, 1)
    group_sums(2)
    partial_sums(0, 0)
    outputs(3, 1)
    group_sums(3)
    partial_sums(1, 0)
    for g in range(2):
        for t in range(2):
            for r in range(2):
                part_copy(t, 2 - 2 * g + r).wait_recv()
            outputs(t, g)
            if g == 1:
                group_sums(t)

    def out_all(t, g, count):
        return pltpu.make_async_remote_copy(
            send.at[t, g, pl.ds(0, count)],
            got.at[t, g, pl.ds(0, count)],
            out_s.at[t, g],
            out_r.at[t, g],
            device_id=(tm, below),
            device_id_type=MESH,
        )

    def arrived(t):
        for g in range(2):
            own_copy(t, g).wait()
            direct = PEERS - 1 - (8 if (t, g) in RELAYED else 0)
            out_all(t, g, direct).wait_send()
            out_all(t, g, PEERS - 1).wait_recv()
        own_sums(t).wait()
        sent = pltpu.make_async_remote_copy(
            got_sums.at[t, pl.ds(0, PEERS - 1)],
            got_sums.at[t, pl.ds(0, PEERS - 1)],
            sum_s.at[t],
            sum_r.at[t],
            device_id=(tm, below),
            device_id_type=MESH,
        )
        sent.wait()

    for n, t in enumerate((2, 3)):
        arrived(t)
        fetch = pltpu.make_async_copy(got.at[t], frame, norm_sem.at[0])
        fetch_sums = pltpu.make_async_copy(got_sums.at[t], frame_sums, norm_sem.at[1])
        fetch.start()
        fetch_sums.start()
        fetch.wait()
        fetch_sums.wait()
        normalize(frame, frame_sums, gain, bias, frame_out.at[n], columns, entries)
        pltpu.make_async_copy(frame_out.at[n], done.at[n], norm_sem.at[2 + n]).start()

    for f in range(FR):
        halo(f).wait_send()
    for n in range(2):
        for row in range(4):
            part_copy(n, row).wait_send()
    for n in range(2):
        pltpu.make_async_copy(frame_out.at[n], done.at[n], norm_sem.at[2 + n]).wait()
    for n in range(len(RELAYED)):
        relay_all(n).wait_send()
        forward_all(n).wait_send()
    arrived(0)
    arrived(1)


def conv_call(clips, frames, weight, gain, bias, entries):
    dma = pltpu.SemaphoreType.DMA
    anywhere = pl.BlockSpec(memory_space=pl.ANY)
    return pl.pallas_call(
        functools.partial(conv_kernel, entries),
        out_shape=[
            jax.ShapeDtypeStruct((FR, 2, PEERS, 2 * COLS, CO), jnp.bfloat16),
            jax.ShapeDtypeStruct((FR, PEERS, 2, CO), jnp.float32),
            jax.ShapeDtypeStruct((2, COLS, PEERS * 4, CO), jnp.bfloat16),
        ],
        in_specs=[
            pl.BlockSpec(memory_space=pltpu.SMEM),
            anywhere,
            anywhere,
            pl.BlockSpec(memory_space=pltpu.VMEM),
            pl.BlockSpec(memory_space=pltpu.VMEM),
        ],
        out_specs=[anywhere] * 3,
        scratch_shapes=[
            pltpu.VMEM((FR, BAND + 1, WIDTH, CI), jnp.bfloat16),
            pltpu.VMEM((FR, BAND + 1, WO, 3 * CI), jnp.bfloat16),
            pltpu.VMEM((3, 9 * CI, CO), jnp.bfloat16),
            pltpu.VMEM((FR, 2, PEERS, 2 * COLS, CO), jnp.bfloat16),
            pltpu.VMEM((2, 4, WO, CO), jnp.bfloat16),
            pltpu.VMEM((2, 4, WO, CO), jnp.bfloat16),
            pltpu.VMEM((FR, 2, 8, CO), jnp.float32),
            pltpu.VMEM((FR, 2, CO), jnp.float32),
            pltpu.VMEM((2, PEERS, 2 * COLS, CO), jnp.bfloat16),
            pltpu.VMEM((PEERS, 2, CO), jnp.float32),
            pltpu.VMEM((2, COLS, PEERS * 4, CO), jnp.bfloat16),
            pltpu.VMEM((2, COLS * PITCH, 128), jnp.float32),
            dma((FR + 1, 2)), dma((FR,)), dma((FR,)), dma((2, 4)), dma((2, 4)),
            dma((FR, 2)), dma((FR, 2)), dma((FR,)), dma((FR,)), dma((FR, 3)), dma((4,)),
            pltpu.VMEM((len(RELAYED), 8, 2 * COLS, CO), jnp.bfloat16),
            dma((len(RELAYED),)), dma((len(RELAYED),)), dma((len(RELAYED),)),
        ],
        compiler_params=pltpu.CompilerParams(
            collective_id=0, has_side_effects=True, vmem_limit_bytes=60 * MIB
        ),
        name="conv",
    )(clips, frames, weight, gain, bias)


def last_kernel(
    entries, got, got_sums, gain, bias, done, latent,
    frame, frame_sums, frame_out, columns, kept, got_sem, sum_sem, out_sem, in_sem, back_sem,
):
    def fetch(t):
        return pltpu.make_async_copy(got.at[t], frame.at[t], got_sem.at[t])

    def fetch_sums(t):
        return pltpu.make_async_copy(got_sums.at[t], frame_sums.at[t], sum_sem.at[t])

    def into(n):
        return pltpu.make_async_copy(done.at[n], kept.at[n], in_sem.at[n])

    def back(n):
        return pltpu.make_async_copy(kept.at[n], latent.at[2 + n], back_sem.at[n])

    def out(t):
        return pltpu.make_async_copy(frame_out.at[t], latent.at[t], out_sem.at[t])

    for t in range(2):
        fetch_sums(t).start()
        fetch(t).start()
    for n in range(2):
        into(n).start()
    for t in range(2):
        fetch_sums(t).wait()
        fetch(t).wait()
        normalize(frame.at[t], frame_sums.at[t], gain, bias, frame_out.at[t], columns, entries)
        out(t).start()
        into(t).wait()
        back(t).start()
    for t in range(2):
        out(t).wait()
        back(t).wait()


def last_call(got, got_sums, gain, bias, done, entries):
    anywhere = pl.BlockSpec(memory_space=pl.ANY)
    inside = pl.BlockSpec(memory_space=pltpu.VMEM)
    return pl.pallas_call(
        functools.partial(last_kernel, entries),
        out_shape=jax.ShapeDtypeStruct((FR, COLS, PEERS * 4, CO), jnp.bfloat16),
        in_specs=[anywhere, anywhere, inside, inside, anywhere],
        out_specs=anywhere,
        scratch_shapes=[
            pltpu.VMEM((2, 2, PEERS, 2 * COLS, CO), jnp.bfloat16),
            pltpu.VMEM((2, PEERS, 2, CO), jnp.float32),
            pltpu.VMEM((2, COLS, PEERS * 4, CO), jnp.bfloat16),
            pltpu.VMEM((2, COLS * PITCH, 128), jnp.float32),
            pltpu.VMEM((2, COLS, PEERS * 4, CO), jnp.bfloat16),
            pltpu.SemaphoreType.DMA((2,)),
            pltpu.SemaphoreType.DMA((2,)),
            pltpu.SemaphoreType.DMA((2,)),
            pltpu.SemaphoreType.DMA((2,)),
            pltpu.SemaphoreType.DMA((2,)),
        ],
        compiler_params=pltpu.CompilerParams(vmem_limit_bytes=60 * MIB),
        name="last",
    )(got, got_sums, gain, bias, done)


def on_device(frames, clip_ids, conv_weight, norm_gain, norm_bias):
    weight = conv_weight.reshape(3, 9 * CI, CO)
    gain, bias = norm_gain.reshape(1, CO), norm_bias.reshape(1, CO)
    entries = float(PEERS * 4 * WO * (CO // GROUPS))
    got, got_sums, done = conv_call(clip_ids, frames, weight, gain, bias, entries)
    latent = last_call(got, got_sums, gain, bias, done, entries)
    return latent.transpose(0, 2, 1, 3)


def solution(mesh):
    in_specs = (P("tm", "rows", None, None), P(), P(), P(), P())
    out_specs = P("tm", None, "rows", None)
    return jax.shard_map(
        on_device, mesh=mesh, in_specs=in_specs, out_specs=out_specs, check_vma=False
    )
```

```python
import functools

import jax
import jax.numpy as jnp
from jax import lax
from jax.experimental import pallas as pl
from jax.experimental.pallas import tpu as pltpu
from jax.sharding import PartitionSpec as P

GROUPS = 32
EPS = 1e-05
MESH = pl.DeviceIdType.MESH
MIB = 2**20
FR = 4
BAND = 8
WIDTH = 1280
WO = 640
CI = 128
CO = 256
COLS = 20
PEERS = 32
TILE = 320
PIECE = 160
PIECES = WIDTH // PIECE
RELAYED = ((2, 0), (3, 0))


def repeat(count, body):
    lax.fori_loop(0, count, lambda u, c: (body(u), c)[1], 0)


PITCH = 136


def group_totals(sums):
    lane = lax.broadcasted_iota(jnp.int32, sums.shape, 1)
    for by in (1, 2, 4):
        up, down = pltpu.roll(sums, CO - by, 1), pltpu.roll(sums, by, 1)
        sums = sums + jnp.where(lax.rem(lane // by, 2) == 0, up, down)
    return sums


def moments(sums, gain, entries):
    total = jnp.sum(sums, axis=0)
    total = group_totals(jnp.concatenate([total, jnp.zeros((6, CO), jnp.float32)], axis=0))
    mean = total[0:1] / entries
    variance = total[1:2] / entries - mean * mean
    return mean, lax.rsqrt(variance + EPS) * gain


def normalize(frame, sums, gain, bias, latent, columns, entries):
    mean, scale = moments(sums[...], gain[...], entries)
    scale = scale * 0.5
    shift = bias[...] * 0.5
    for s in range(PEERS):
        for g in range(2):
            half = (frame[g, s].astype(jnp.float32) - mean) * scale + shift
            value = half * jnp.tanh(half) + half
            for r in range(2):
                for h in range(2):
                    columns[h, pl.ds(4 * s + 2 - 2 * g + r, COLS, stride=PITCH), :] = value[
                        r * COLS : (r + 1) * COLS, h * 128 : (h + 1) * 128
                    ]
    for j in range(COLS):
        for h in range(2):
            latent[j, :, h * 128 : (h + 1) * 128] = columns[
                h, pl.ds(j * PITCH, 4 * PEERS), :
            ].astype(jnp.bfloat16)


def conv_kernel(
    entries, clips, frames, weight_in, gain, bias, got, got_sums, done,
    rows_in, taps_in, weight, send, part_send, part_got, sums, sums_send,
    frame, frame_sums, frame_out, columns,
    load_sem, halo_s, halo_r, part_s, part_r, out_s, out_r, sum_s, sum_r, own_sem, norm_sem, relay, relay_s, relay_r, forward_s,
):
    tm = lax.axis_index("tm")
    me = lax.axis_index("rows")
    tm_count = lax.axis_size("tm")
    tm_next = lax.rem(tm + 1, tm_count)
    tm_last = lax.rem(tm + tm_count - 1, tm_count)
    below = lax.rem(me + 1, PEERS)

    def load(f, part):
        first, count = ((3, 5), (0, 3))[part]
        return pltpu.make_async_copy(
            frames.at[f, pl.ds(first, count)],
            rows_in.at[f, pl.ds(first + 1, count)],
            load_sem.at[f, part],
        )

    load_weight = pltpu.make_async_copy(weight_in, weight, load_sem.at[FR, 0])
    load(2, 0).start()
    load(3, 0).start()
    load_weight.start()
    load(0, 0).start()
    load(1, 0).start()
    for f in (2, 3, 0, 1):
        load(f, 1).start()

    barrier = pltpu.get_barrier_semaphore()

    def greet(d):
        to = lax.rem(me + 1 + d, PEERS)
        pl.semaphore_signal(barrier, inc=1, device_id=(tm, to), device_id_type=MESH)

    repeat(PEERS - 1, greet)
    for other in (tm_next, tm_last):
        pl.semaphore_signal(barrier, inc=1, device_id=(other, me), device_id_type=MESH)

    sums[...] = jnp.zeros(sums.shape, jnp.float32)
    above = jnp.where(me > 0, 1.0, 0.0).astype(jnp.bfloat16)

    def split(f, first, count):
        def body(u):
            r = first + u
            row = rows_in[f, r]
            pairs = (row if first else row * above).reshape(WO, 2 * CI)
            taps_in[f, r, :, CI:] = pairs
            before = jnp.zeros((1, CI), jnp.bfloat16)
            taps_in[f, r, :, :CI] = jnp.concatenate([before, pairs[:-1, CI:]], axis=0)

        repeat(count, body)

    start = tm * FR

    def mask(target, source):
        inside = jnp.logical_or(tm < tm_count - 1, target < FR)
        last = tm_count * FR
        same = clips[lax.rem(start + target, last)] == clips[lax.rem(start + source, last)]
        return jnp.where(jnp.logical_and(inside, same), 1.0, 0.0).astype(jnp.float32)

    def dots(terms, row, col):
        total = None
        for f, k, m in terms:
            left = jnp.concatenate(
                [taps_in[f, 2 * row + a, pl.ds(col, TILE), :] for a in range(3)], axis=1
            )
            term = jnp.dot(left, weight[k], preferred_element_type=jnp.float32)
            if m is not None:
                term = term * m
            total = term if total is None else total + term
        return total

    def halo(f):
        return pltpu.make_async_remote_copy(
            frames.at[f, BAND - 1],
            rows_in.at[f, 0],
            halo_s.at[f],
            halo_r.at[f],
            device_id=(tm, below),
            device_id_type=MESH,
        )

    def halo_pieces(first, count):
        def body(u):
            i = first + u
            f = lax.rem(i // PIECES * 2, 4) + i // (2 * PIECES)
            at = pl.ds(pl.multiple_of(lax.rem(i, PIECES) * PIECE, PIECE), PIECE)
            pltpu.make_async_remote_copy(
                frames.at[f, BAND - 1, at],
                rows_in.at[f, 0, at],
                halo_s.at[f],
                halo_r.at[f],
                device_id=(tm, below),
                device_id_type=MESH,
            ).start()

        repeat(count, body)

    def part_copy(n, row):
        return pltpu.make_async_remote_copy(
            part_send.at[n, row],
            part_got.at[n, row],
            part_s.at[n, row],
            part_r.at[n, row],
            device_id=(tm_next, me),
            device_id_type=MESH,
        )

    def partial_sums(n, row):
        if n == 0:
            terms = [(2, 0, mask(4, 2)), (3, 1, mask(4, 3))]
        else:
            terms = [(3, 0, mask(5, 3))]

        def body(q):
            col = pl.multiple_of(q * TILE, TILE)
            part_send[n, row, pl.ds(col, TILE), :] = dots(terms, row, col).astype(jnp.bfloat16)

        repeat(2, body)
        part_copy(n, row).start()

    def out_copy(t, g, to):
        return pltpu.make_async_remote_copy(
            send.at[t, g, to],
            got.at[t, g, me],
            out_s.at[t, g],
            out_r.at[t, g],
            device_id=(tm, to),
            device_id_type=MESH,
        )

    y, z, core = me // 8, lax.rem(me // 2, 4), lax.rem(me, 2)
    z_less, z_more, z_two = lax.rem(z + 3, 4), lax.rem(z + 1, 4), lax.rem(z + 2, 4)

    def relay_copy(n, d):
        t, g = RELAYED[n]
        to = lax.rem(y + d // 2, 4) * 8 + z_two * 2 + lax.rem(core + d, 2)
        return pltpu.make_async_remote_copy(
            send.at[t, g, to],
            relay.at[n, d],
            relay_s.at[n],
            relay_r.at[n],
            device_id=(tm, y * 8 + z_less * 2 + core),
            device_id_type=MESH,
        )

    def forward(n):
        t, g = RELAYED[n]
        source = y * 8 + z_more * 2 + core
        relay_all(n).wait_recv()

        def body(d):
            to = lax.rem(y + d // 2, 4) * 8 + z_less * 2 + lax.rem(core + d, 2)
            pltpu.make_async_remote_copy(
                relay.at[n, d],
                got.at[t, g, source],
                forward_s.at[n],
                out_r.at[t, g],
                device_id=(tm, to),
                device_id_type=MESH,
            ).start()

        repeat(8, body)

    def relay_all(n):
        return pltpu.make_async_remote_copy(
            relay.at[n], relay.at[n], relay_s.at[n], relay_r.at[n],
            device_id=(tm, below), device_id_type=MESH,
        )

    def forward_all(n):
        return pltpu.make_async_remote_copy(
            relay.at[n], relay.at[n], forward_s.at[n], relay_r.at[n],
            device_id=(tm, below), device_id_type=MESH,
        )

    def own_copy(t, g):
        return pltpu.make_async_copy(send.at[t, g, me], got.at[t, g, me], own_sem.at[t, g])

    def outputs(t, g):
        terms = [
            (t - 2 + k, k, None if k == 2 else mask(t, t - 2 + k)) for k in range(3) if t - 2 + k >= 0
        ]
        row = 2 - 2 * g
        pairs = TILE // (2 * COLS)

        def body(u):
            q = u
            col = pl.multiple_of(q * TILE, TILE)
            upper = dots(terms, row, col)
            lower = dots(terms, row + 1, col)
            if t < 2:
                upper = upper + part_got[t, row, pl.ds(col, TILE), :].astype(jnp.float32)
                lower = lower + part_got[t, row + 1, pl.ds(col, TILE), :].astype(jnp.float32)
            by8 = (TILE // 8, 8, CO)
            sums[t, 0] += jnp.sum((upper + lower).reshape(by8), axis=0)
            sums[t, 1] += jnp.sum((upper * upper + lower * lower).reshape(by8), axis=0)
            upper = upper.reshape(pairs, 2 * COLS, CO)
            lower = lower.reshape(pairs, 2 * COLS, CO)
            even = jnp.concatenate([upper[:, :COLS], lower[:, :COLS]], axis=1)
            odd = jnp.concatenate([upper[:, COLS:], lower[:, COLS:]], axis=1)
            for j in range(pairs):
                to = q * (2 * pairs) + 2 * j
                send[t, g, to] = even[j].astype(jnp.bfloat16)
                send[t, g, to + 1] = odd[j].astype(jnp.bfloat16)

        def push(d):
            step = lax.rem(11 * d + 5, PEERS)
            far = lax.rem(step // 2, 4)
            to = lax.rem(y + step // 8, 4) * 8 + lax.rem(z + far, 4) * 2 + lax.rem(core + step, 2)
            direct = step != 0
            if (t, g) in RELAYED:
                direct = jnp.logical_and(direct, far != 2)

            @pl.when(direct)
            def _():
                out_copy(t, g, to).start()

        repeat(2, body)
        if (t, g) in RELAYED:
            repeat(8, lambda d: relay_copy(RELAYED.index((t, g)), d).start())
        repeat(PEERS, push)
        own_copy(t, g).start()

    def sum_copy(t, to):
        return pltpu.make_async_remote_copy(
            sums_send.at[t],
            got_sums.at[t, me],
            sum_s.at[t],
            sum_r.at[t],
            device_id=(tm, to),
            device_id_type=MESH,
        )

    def own_sums(t):
        return pltpu.make_async_copy(sums_send.at[t], got_sums.at[t, me], own_sem.at[t, 2])

    def group_sums(t):
        sums_send[t] = jnp.sum(sums[t], axis=1)
        repeat(PEERS - 1, lambda d: sum_copy(t, lax.rem(me + 1 + d, PEERS)).start())
        own_sums(t).start()

    pl.semaphore_wait(barrier, PEERS + 1)
    halo_pieces(0, 32)
    for f in (2, 3):
        load(f, 0).wait()
        split(f, 4, 5)
    load_weight.wait()
    partial_sums(0, 2)
    for f in (0, 1):
        load(f, 0).wait()
        split(f, 4, 5)
    outputs(2, 0)
    partial_sums(0, 3)
    outputs(3, 0)
    partial_sums(1, 2)
    partial_sums(1, 3)
    for f in (2, 3):
        load(f, 1).wait()
        split(f, 1, 3)
    partial_sums(0, 1)
    partial_sums(1, 1)
    for f in (0, 1):
        load(f, 1).wait()
        split(f, 1, 3)
    for f in (0, 2, 1, 3):
        halo(f).wait_recv()
    for n in range(len(RELAYED)):
        forward(n)
    for f in (0, 1, 2, 3):
        split(f, 0, 1)
    outputs(2, 1)
    group_sums(2)
    partial_sums(0, 0)
    outputs(3, 1)
    group_sums(3)
    partial_sums(1, 0)
    for g in range(2):
        for t in range(2):
            for r in range(2):
                part_copy(t, 2 - 2 * g + r).wait_recv()
            outputs(t, g)
            if g == 1:
                group_sums(t)

    def out_all(t, g, count):
        return pltpu.make_async_remote_copy(
            send.at[t, g, pl.ds(0, count)],
            got.at[t, g, pl.ds(0, count)],
            out_s.at[t, g],
            out_r.at[t, g],
            device_id=(tm, below),
            device_id_type=MESH,
        )

    def arrived(t):
        for g in range(2):
            own_copy(t, g).wait()
            direct = PEERS - 1 - (8 if (t, g) in RELAYED else 0)
            out_all(t, g, direct).wait_send()
            out_all(t, g, PEERS - 1).wait_recv()
        own_sums(t).wait()
        sent = pltpu.make_async_remote_copy(
            got_sums.at[t, pl.ds(0, PEERS - 1)],
            got_sums.at[t, pl.ds(0, PEERS - 1)],
            sum_s.at[t],
            sum_r.at[t],
            device_id=(tm, below),
            device_id_type=MESH,
        )
        sent.wait()

    for n, t in enumerate((2, 3)):
        arrived(t)
        fetch = pltpu.make_async_copy(got.at[t], frame, norm_sem.at[0])
        fetch_sums = pltpu.make_async_copy(got_sums.at[t], frame_sums, norm_sem.at[1])
        fetch.start()
        fetch_sums.start()
        fetch.wait()
        fetch_sums.wait()
        normalize(frame, frame_sums, gain, bias, frame_out.at[n], columns, entries)
        pltpu.make_async_copy(frame_out.at[n], done.at[n], norm_sem.at[2 + n]).start()

    for f in range(FR):
        halo(f).wait_send()
    for n in range(2):
        for row in range(4):
            part_copy(n, row).wait_send()
    for n in range(2):
        pltpu.make_async_copy(frame_out.at[n], done.at[n], norm_sem.at[2 + n]).wait()
    for n in range(len(RELAYED)):
        relay_all(n).wait_send()
        forward_all(n).wait_send()
    arrived(0)
    arrived(1)


def conv_call(clips, frames, weight, gain, bias, entries):
    dma = pltpu.SemaphoreType.DMA
    anywhere = pl.BlockSpec(memory_space=pl.ANY)
    return pl.pallas_call(
        functools.partial(conv_kernel, entries),
        out_shape=[
            jax.ShapeDtypeStruct((FR, 2, PEERS, 2 * COLS, CO), jnp.bfloat16),
            jax.ShapeDtypeStruct((FR, PEERS, 2, CO), jnp.float32),
            jax.ShapeDtypeStruct((2, COLS, PEERS * 4, CO), jnp.bfloat16),
        ],
        in_specs=[
            pl.BlockSpec(memory_space=pltpu.SMEM),
            anywhere,
            anywhere,
            pl.BlockSpec(memory_space=pltpu.VMEM),
            pl.BlockSpec(memory_space=pltpu.VMEM),
        ],
        out_specs=[anywhere] * 3,
        scratch_shapes=[
            pltpu.VMEM((FR, BAND + 1, WIDTH, CI), jnp.bfloat16),
            pltpu.VMEM((FR, BAND + 1, WO, 3 * CI), jnp.bfloat16),
            pltpu.VMEM((3, 9 * CI, CO), jnp.bfloat16),
            pltpu.VMEM((FR, 2, PEERS, 2 * COLS, CO), jnp.bfloat16),
            pltpu.VMEM((2, 4, WO, CO), jnp.bfloat16),
            pltpu.VMEM((2, 4, WO, CO), jnp.bfloat16),
            pltpu.VMEM((FR, 2, 8, CO), jnp.float32),
            pltpu.VMEM((FR, 2, CO), jnp.float32),
            pltpu.VMEM((2, PEERS, 2 * COLS, CO), jnp.bfloat16),
            pltpu.VMEM((PEERS, 2, CO), jnp.float32),
            pltpu.VMEM((2, COLS, PEERS * 4, CO), jnp.bfloat16),
            pltpu.VMEM((2, COLS * PITCH, 128), jnp.float32),
            dma((FR + 1, 2)), dma((FR,)), dma((FR,)), dma((2, 4)), dma((2, 4)),
            dma((FR, 2)), dma((FR, 2)), dma((FR,)), dma((FR,)), dma((FR, 3)), dma((4,)),
            pltpu.VMEM((len(RELAYED), 8, 2 * COLS, CO), jnp.bfloat16),
            dma((len(RELAYED),)), dma((len(RELAYED),)), dma((len(RELAYED),)),
        ],
        compiler_params=pltpu.CompilerParams(
            collective_id=0, has_side_effects=True, vmem_limit_bytes=60 * MIB
        ),
        name="conv",
    )(clips, frames, weight, gain, bias)


def last_kernel(
    entries, got, got_sums, gain, bias, done, latent,
    frame, frame_sums, frame_out, columns, kept, got_sem, sum_sem, out_sem, in_sem, back_sem,
):
    def fetch(t):
        return pltpu.make_async_copy(got.at[t], frame.at[t], got_sem.at[t])

    def fetch_sums(t):
        return pltpu.make_async_copy(got_sums.at[t], frame_sums.at[t], sum_sem.at[t])

    def into(n):
        return pltpu.make_async_copy(done.at[n], kept.at[n], in_sem.at[n])

    def back(n):
        return pltpu.make_async_copy(kept.at[n], latent.at[2 + n], back_sem.at[n])

    def out(t):
        return pltpu.make_async_copy(frame_out.at[t], latent.at[t], out_sem.at[t])

    for t in range(2):
        fetch_sums(t).start()
        fetch(t).start()
    for n in range(2):
        into(n).start()
    for t in range(2):
        fetch_sums(t).wait()
        fetch(t).wait()
        normalize(frame.at[t], frame_sums.at[t], gain, bias, frame_out.at[t], columns, entries)
        out(t).start()
        into(t).wait()
        back(t).start()
    for t in range(2):
        out(t).wait()
        back(t).wait()


def last_call(got, got_sums, gain, bias, done, entries):
    anywhere = pl.BlockSpec(memory_space=pl.ANY)
    inside = pl.BlockSpec(memory_space=pltpu.VMEM)
    return pl.pallas_call(
        functools.partial(last_kernel, entries),
        out_shape=jax.ShapeDtypeStruct((FR, COLS, PEERS * 4, CO), jnp.bfloat16),
        in_specs=[anywhere, anywhere, inside, inside, anywhere],
        out_specs=anywhere,
        scratch_shapes=[
            pltpu.VMEM((2, 2, PEERS, 2 * COLS, CO), jnp.bfloat16),
            pltpu.VMEM((2, PEERS, 2, CO), jnp.float32),
            pltpu.VMEM((2, COLS, PEERS * 4, CO), jnp.bfloat16),
            pltpu.VMEM((2, COLS * PITCH, 128), jnp.float32),
            pltpu.VMEM((2, COLS, PEERS * 4, CO), jnp.bfloat16),
            pltpu.SemaphoreType.DMA((2,)),
            pltpu.SemaphoreType.DMA((2,)),
            pltpu.SemaphoreType.DMA((2,)),
            pltpu.SemaphoreType.DMA((2,)),
            pltpu.SemaphoreType.DMA((2,)),
        ],
        compiler_params=pltpu.CompilerParams(vmem_limit_bytes=60 * MIB),
        name="last",
    )(got, got_sums, gain, bias, done)


def on_device(frames, clip_ids, conv_weight, norm_gain, norm_bias):
    weight = conv_weight.reshape(3, 9 * CI, CO)
    gain, bias = norm_gain.reshape(1, CO), norm_bias.reshape(1, CO)
    entries = float(PEERS * 4 * WO * (CO // GROUPS))
    got, got_sums, done = conv_call(clip_ids, frames, weight, gain, bias, entries)
    latent = last_call(got, got_sums, gain, bias, done, entries)
    return latent.transpose(0, 2, 1, 3)


def solution(mesh):
    in_specs = (P("tm", "rows", None, None), P(), P(), P(), P())
    out_specs = P("tm", None, "rows", None)
    return jax.shard_map(
        on_device, mesh=mesh, in_specs=in_specs, out_specs=out_specs, check_vma=False
    )
```
